32 devices in a mesh: grp: 2 (over y), row: 4 (over z), view: 2 (over x), col: 2 (over core).
Axes of the slice: x: 2, y: 2, z: 4, core: 2. Of those that a mesh axis runs over, the one named last changes fastest.
Arguments:
- omega: bfloat16 [16384, 256], P('row', 'col'), may hold values from -6 to 6
- neighbor_ids: int32 [2, 10, 32768], P('view', None, ('grp', 'row')), parts along dimension 2, may hold values from 0 to 1151
- degrees: int32 [2, 32768], P('view', ('grp', 'row')), parts along dimension 1, may hold values from 10 to 39
Outputs:
- basis: float32 [32768, 256], P(('grp', 'row', 'view'), 'col'), parts along dimension 0
- factor: float32 [512, 256], P('grp', 'col'), parts along dimension 0
The draws below stay inside these ranges and needn't reach their ends.
There are 2 independent parts, one for each index of `grp`. The reference program is written for one: setup_inputs(seed, part) draws one part's arguments, and reference() takes and returns one part's arrays. A program takes and returns all parts, laid end to end along the dimension named above; an argument that names none is the same for every part. Nothing has to cross between parts.
All inputs are finite; a program needn't handle non-finite values.
Results may differ from the reference program's by a relative error of at most 0.0052.
Values may be sent and summed in bfloat16 or wider, within the bound.
A program may use at most 64 MiB of HBM per device.

```python
import math
import jax
import jax.numpy as jnp
from jax import lax

TILE = 128
BAND = 4
NNZ = 10
K = 256
VIEWS = 2
NROWS = 16384


def set_ends(array, key, smallest, largest):
    longest = array.shape.index(max(array.shape))
    spots = []
    for shift in (0, 1):
        where = [jax.random.randint(jax.random.fold_in(key, axis), (), 0, length) for axis, length in enumerate(array.shape)]
        where[longest] = (where[longest] + shift) % array.shape[longest]
        spots.append(tuple(where))
    return array.at[spots[0]].set(smallest).at[spots[1]].set(largest)


def steps_of(own_key, extent, cuts, least, top_value):
    def one(dim, blocks):
        draws = jax.random.uniform(jax.random.fold_in(jax.random.fold_in(own_key, 6), dim), (blocks,), jnp.float32, least / len(cuts), top_value / len(cuts))
        return jnp.repeat(jnp.exp(draws), extent[dim] // blocks).reshape((-1,) + (1,) * (len(extent) - dim - 1))

    level = one(*cuts[0])
    for cut in cuts[1:]:
        level = level * one(*cut)
    return level


def normal_values(key, dims, spread, bound, cuts=(), kind=jnp.bfloat16):
    factor_of = steps_of(key, dims, cuts, -0.22, 0.18) if cuts else 1.0
    array = jax.random.normal(key, dims, jnp.float32) * spread * factor_of
    return jnp.minimum(jnp.maximum(array, -bound), bound).astype(kind)


def setup_inputs(seed: int = 0, part: int = 0) -> dict:
    key_list = jax.random.split(jax.random.key(seed), 4)
    own_keys = jax.random.split(jax.random.fold_in(key_list[3], part), 4)
    omega = normal_values(key_list[0], (NROWS, K), 1.0, 6.0, ((0, 4), (1, 2)))
    neighbor_ids = set_ends(jax.random.randint(own_keys[1], (VIEWS, NNZ, NROWS), 0, (2 * BAND + 1) * TILE), jax.random.fold_in(own_keys[1], 1), 0, ((2 * BAND + 1) * TILE) - 1).astype(jnp.int32)
    degrees = set_ends(jax.random.randint(own_keys[2], (VIEWS, NROWS), NNZ, 4 * NNZ), jax.random.fold_in(own_keys[2], 1), NNZ, (4 * NNZ) - 1).astype(jnp.int32)
    return dict(omega=omega, neighbor_ids=neighbor_ids, degrees=degrees)


def apply_view(sketch, window_ids, inv_root):
    row_count = sketch.shape[0]
    tile_count = row_count // TILE
    scaled = (inv_root[:, None] * sketch.astype(jnp.float32)).astype(jnp.bfloat16)
    padded = jnp.pad(scaled, ((BAND * TILE, BAND * TILE), (0, 0)))
    tiled_ids = window_ids.reshape(NNZ, tile_count, TILE)
    positions = jnp.arange(TILE, dtype=jnp.int32)
    result = jnp.zeros((tile_count, TILE, sketch.shape[1]), jnp.float32)
    for offset in range(2 * BAND + 1):
        counts = jnp.zeros((tile_count, TILE, TILE), jnp.float32)
        for slot_index in range(NNZ):
            counts = counts + (tiled_ids[slot_index][:, :, None] == offset * TILE + positions).astype(jnp.float32)
        shifted = padded[offset * TILE:offset * TILE + row_count].astype(jnp.float32).reshape(tile_count, TILE, -1)
        result = result + jnp.einsum('tij,tjc->tic', counts, shifted)
    return inv_root[:, None] * result.reshape(row_count, -1)

def reference(omega, neighbor_ids, degrees):
    inv_root = 1.0 / jnp.sqrt(degrees.astype(jnp.float32))
    first = jnp.zeros((NROWS, K), jnp.float32)
    for view_index in range(VIEWS):
        first = first + apply_view(omega, neighbor_ids[view_index], inv_root[view_index])
    first = first.astype(jnp.bfloat16)
    second = jnp.zeros((NROWS, K), jnp.float32)
    for view_index in range(VIEWS):
        second = second + apply_view(first, neighbor_ids[view_index], inv_root[view_index])
    gram_matrix = jnp.einsum('rk,rj->kj', second, second, precision=lax.Precision.HIGHEST)
    lower_factor = jnp.linalg.cholesky(gram_matrix)
    row_scale = math.sqrt(NROWS)
    solved = jax.scipy.linalg.solve_triangular(lower_factor, second.T, lower=True)
    basis = solved.T * row_scale
    factor = lower_factor.T / row_scale
    return (basis, factor)
```

```python
import functools
import math

import jax
import jax.numpy as jnp
from jax import lax
from jax.experimental import pallas as pl
from jax.experimental.pallas import tpu as pltpu
from jax.sharding import PartitionSpec as P

TILE = 128
BAND = 4
HALO = TILE * BAND
PAIR = 2 * TILE
SPAN = PAIR + 2 * HALO
FIELDS = SPAN // TILE
BLOCK = 32
MESH = pl.DeviceIdType.MESH
HIGHEST = lax.Precision.HIGHEST


def sketch_kernel(
    zs, vs, omega_ref, ids_ref, deg_ref, both_ref, gram_ref,
    om, ids, deg, inv, counts, scaled, first,
    local_sems, ids_sems, deg_sems, om_sems, edge_sems, edge_deg_sems, halo_sems, both_sems,
):
    grp, r, v, c = (lax.axis_index(a) for a in ("grp", "row", "view", "col"))
    total = zs * vs * 2
    length = omega_ref.shape[0]
    own = length // (2 * vs)
    wide = own + 2 * HALO
    slots = ids_ref.shape[1]
    half = omega_ref.shape[1]
    place = (r * vs + v) * 2 + c
    base = pl.multiple_of((v * 2 + c) * own, HALO)

    def at(index):
        return (grp, index // (2 * vs), (index // 2) % vs, index % 2)

    def remote(src, dst, sems, slot_index, device):
        return pltpu.make_async_remote_copy(
            src_ref=src, dst_ref=dst, send_sem=sems.at[0, slot_index], recv_sem=sems.at[1, slot_index],
            device_id=device, device_id_type=MESH,
        )

    own_ids = pltpu.make_async_copy(ids_ref.at[0, :, pl.ds(base, own)], ids.at[0], local_sems.at[0])
    own_deg = pltpu.make_async_copy(deg_ref, deg.at[0, :, pl.ds(HALO, length)], local_sems.at[1])
    own_om = pltpu.make_async_copy(omega_ref, om.at[c, pl.ds(HALO, length), :], local_sems.at[2])
    own_ids.start()
    own_deg.start()
    own_om.start()

    barrier = pltpu.get_barrier_semaphore()

    def greet(i, carry):
        pl.semaphore_signal(barrier, inc=1, device_id=at((place + i) % total), device_id_type=MESH)
        return carry

    lax.fori_loop(1, total, greet, 0)
    pl.semaphore_wait(barrier, total - 1)

    sends = []
    for k in range(1, vs):
        w = (v + vs - k) % vs
        there = (grp, r, w, c)
        piece = pl.multiple_of((w * 2 + c) * own, HALO)
        sends.append(remote(ids_ref.at[0, :, pl.ds(piece, own)], ids.at[k], ids_sems, k - 1, there))
        sends.append(remote(deg_ref, deg.at[k, :, pl.ds(HALO, length)], deg_sems, k - 1, there))
    window = min(wide, length)
    other_base = (v * 2 + 1 - c) * own
    start = pl.multiple_of(jnp.clip(other_base - HALO, 0, length - window), HALO)
    om_copy = remote(
        omega_ref.at[pl.ds(start, window), :], om.at[c, pl.ds(HALO + start, window), :],
        om_sems, 0, (grp, r, v, 1 - c),
    )
    my_start = pl.multiple_of(jnp.clip(base - HALO, 0, length - window), HALO)
    om_arrive = remote(
        omega_ref.at[pl.ds(start, window), :], om.at[1 - c, pl.ds(HALO + my_start, window), :],
        om_sems, 0, (grp, r, v, 1 - c),
    )
    up_ok = r < zs - 1
    down_ok = r > 0
    next_row = jnp.minimum(r + 1, zs - 1)
    prev_row = jnp.maximum(r - 1, 0)
    low, high = pl.ds(0, HALO), pl.ds(HALO + length, HALO)
    last = pl.ds(length - HALO, HALO)
    firsts = pl.ds(0, HALO)
    edge_up = remote(omega_ref.at[last, :], om.at[c, low, :], edge_sems, c, (grp, next_row, 0, 0))
    edge_down = remote(omega_ref.at[firsts, :], om.at[c, high, :], edge_sems, c, (grp, prev_row, vs - 1, 1))
    slot_up = v
    slot_down = (v + 1) % vs
    deg_up = remote(deg_ref.at[:, last], deg.at[slot_up, :, low], edge_deg_sems, slot_up, (grp, next_row, 0, 0))
    deg_down = remote(
        deg_ref.at[:, firsts], deg.at[slot_down, :, high], edge_deg_sems, slot_down, (grp, prev_row, vs - 1, 1)
    )
    send_edge_up = up_ok & (v == 0)
    send_edge_down = down_ok & (v == vs - 1)
    send_deg_up = up_ok & (c == 0)
    send_deg_down = down_ok & (c == 1)
    get_low = down_ok & (v == 0) & (c == 0)
    get_high = up_ok & (v == vs - 1) & (c == 1)

    pl.when(send_edge_up)(edge_up.start)
    pl.when(send_edge_down)(edge_down.start)
    for s in sends:
        s.start()
    pl.when(send_deg_up)(deg_up.start)
    pl.when(send_deg_down)(deg_down.start)
    om_copy.start()

    @pl.when(r == 0)
    def _():
        om[:, low, :] = jnp.zeros((2, HALO, half), om.dtype)
        deg[:, :, low] = jnp.ones((vs, 1, HALO), deg.dtype)

    @pl.when(r == zs - 1)
    def _():
        om[:, high, :] = jnp.zeros((2, HALO, half), om.dtype)
        deg[:, :, high] = jnp.ones((vs, 1, HALO), deg.dtype)

    def build(k):
        def one(d, carry):
            mine = ids[k, :, pl.ds(pl.multiple_of(d * PAIR, PAIR), PAIR)]
            lane = lax.broadcasted_iota(jnp.int32, mine.shape, 1)
            tile = (mine >> 7) + jnp.where(lane >= TILE, 1, 0)
            within = mine & (TILE - 1)
            one_a = jnp.where(tile < 8, jnp.int32(1) << (4 * jnp.minimum(tile, 7)), 0)
            one_b = jnp.where(tile >= 8, jnp.int32(1) << (4 * jnp.maximum(tile - 8, 0)), 0)
            rows = 32
            for p in range(TILE // rows):
                spot = lax.broadcasted_iota(jnp.int32, (rows, PAIR), 0) + p * rows
                acc_a = jnp.zeros((rows, PAIR), jnp.int32)
                acc_b = jnp.zeros((rows, PAIR), jnp.int32)
                for s in range(slots):
                    hit = within[s : s + 1, :] == spot
                    acc_a = acc_a + jnp.where(hit, one_a[s : s + 1, :], 0)
                    acc_b = acc_b + jnp.where(hit, one_b[s : s + 1, :], 0)
                for h in range(FIELDS):
                    acc = acc_a if h < 8 else acc_b
                    field = (acc >> (4 * (h % 8))) & 15
                    counts[k, d, h * TILE + p * rows : h * TILE + (p + 1) * rows, :] = field.astype(
                        jnp.float32
                    ).astype(jnp.bfloat16)
            return carry

        lax.fori_loop(0, own // PAIR, one, 0)

    own_ids.wait()
    build(0)
    for k in range(1, vs):
        sends[2 * (k - 1)].wait_recv()
        build(k)
    for k in range(1, vs):
        sends[2 * (k - 1) + 1].wait_recv()
    own_deg.wait()
    own_om.wait()
    om_arrive.wait_recv()

    @pl.when(get_low)
    def _():
        for h in range(2):
            remote(omega_ref.at[last, :], om.at[h, low, :], edge_sems, h, (grp, prev_row, 0, 0)).wait_recv()
        for k in range(vs):
            remote(deg_ref.at[:, last], deg.at[k, :, low], edge_deg_sems, k, (grp, prev_row, 0, 0)).wait_recv()

    @pl.when(get_high)
    def _():
        for h in range(2):
            remote(omega_ref.at[firsts, :], om.at[h, high, :], edge_sems, h, (grp, next_row, 0, 0)).wait_recv()
        for k in range(vs):
            remote(deg_ref.at[:, firsts], deg.at[k, :, high], edge_deg_sems, k, (grp, next_row, 0, 0)).wait_recv()

    for k in range(vs):
        inv[k] = 1.0 / jnp.sqrt(deg[k, :, pl.ds(base, wide)].astype(jnp.float32))

    def turn(i, carry):
        lanes = pl.ds(pl.multiple_of(i * PAIR, PAIR), PAIR)
        for h in range(2):
            part = om[h, pl.ds(pl.multiple_of(base + i * PAIR, PAIR), PAIR), :].astype(jnp.float32).T
            for k in range(vs):
                scaled[k, h * half : (h + 1) * half, lanes] = (inv[k, :, lanes] * part).astype(jnp.bfloat16)
        return carry

    lax.fori_loop(0, wide // PAIR, turn, 0)

    def product(d):
        out = None
        for k in range(vs):
            term = jnp.dot(
                scaled[k, :, pl.ds(pl.multiple_of(d * PAIR, PAIR), SPAN)], counts[k, d],
                preferred_element_type=jnp.float32,
            )
            term = inv[k, :, pl.ds(pl.multiple_of(HALO + d * PAIR, PAIR), PAIR)] * term
            out = term if out is None else out + term
        return out

    def sweep_one(d, carry):
        first[:, pl.ds(pl.multiple_of(HALO + d * PAIR, PAIR), PAIR)] = product(d).astype(jnp.bfloat16)
        return carry

    before = at(jnp.maximum(place - 1, 0))
    after = at(jnp.minimum(place + 1, total - 1))
    down = remote(first.at[:, pl.ds(HALO, HALO)], first.at[:, pl.ds(HALO + own, HALO)], halo_sems, 0, before)
    up = remote(first.at[:, pl.ds(own, HALO)], first.at[:, pl.ds(0, HALO)], halo_sems, 1, after)
    has_before, has_after = place > 0, place < total - 1

    lax.fori_loop(0, HALO // PAIR, sweep_one, 0)
    pl.when(has_before)(down.start)
    lax.fori_loop(HALO // PAIR, own // PAIR, sweep_one, 0)
    pl.when(has_after)(up.start)

    @pl.when(place == 0)
    def _():
        first[:, pl.ds(0, HALO)] = jnp.zeros((2 * half, HALO), first.dtype)

    @pl.when(place == total - 1)
    def _():
        first[:, pl.ds(HALO + own, HALO)] = jnp.zeros((2 * half, HALO), first.dtype)

    def rescale(i, carry):
        lanes = pl.ds(pl.multiple_of(i * PAIR, PAIR), PAIR)
        part = first[:, lanes].astype(jnp.float32)
        for k in range(vs):
            scaled[k, :, lanes] = (inv[k, :, lanes] * part).astype(jnp.bfloat16)
        return carry

    lax.fori_loop(HALO // PAIR, (HALO + own) // PAIR, rescale, 0)
    pl.when(has_before)(up.wait_recv)
    lax.fori_loop(0, HALO // PAIR, rescale, 0)
    pl.when(has_after)(down.wait_recv)
    lax.fori_loop((HALO + own) // PAIR, wide // PAIR, rescale, 0)

    def sweep_two(d, carry):
        both_ref[:, pl.ds(pl.multiple_of(c * own + d * PAIR, PAIR), PAIR)] = product(d)
        return carry

    lax.fori_loop(0, own // PAIR, sweep_two, 0)
    mine = pl.ds(pl.multiple_of(c * own, PAIR), own)
    theirs = pl.ds(pl.multiple_of((1 - c) * own, PAIR), own)
    swap = remote(both_ref.at[:, mine], both_ref.at[:, mine], both_sems, 0, (grp, r, v, 1 - c))
    swap_in = remote(both_ref.at[:, mine], both_ref.at[:, theirs], both_sems, 0, (grp, r, v, 1 - c))
    swap.start()
    second = both_ref[:, mine]
    gram_ref[...] = lax.dot_general(
        second, second, (((1,), (1,)), ((), ())), precision=HIGHEST, preferred_element_type=jnp.float32
    )

    swap.wait_send()
    swap_in.wait_recv()
    for s in sends:
        s.wait_send()
    om_copy.wait_send()
    pl.when(send_edge_up)(edge_up.wait_send)
    pl.when(send_edge_down)(edge_down.wait_send)
    pl.when(send_deg_up)(deg_up.wait_send)
    pl.when(send_deg_down)(deg_down.wait_send)
    pl.when(has_before)(down.wait_send)
    pl.when(has_after)(up.wait_send)


def factor_kernel(scale, gram_ref, both_ref, basis_ref, factor_ref, work, upper, inverse):
    size = gram_ref.shape[0]
    c = lax.axis_index("col")
    half = size // 2
    work[:, :size] = gram_ref[...]
    work[:, size:] = jnp.where(
        lax.broadcasted_iota(jnp.int32, (size, size), 0) == lax.broadcasted_iota(jnp.int32, (size, size), 1),
        jnp.float32(1), jnp.float32(0),
    )
    rows = lax.broadcasted_iota(jnp.int32, (BLOCK, BLOCK), 0)
    cols = lax.broadcasted_iota(jnp.int32, (BLOCK, BLOCK), 1)
    for k in range(size // BLOCK):
        lo, hi = k * BLOCK, (k + 1) * BLOCK
        block = work[lo:hi, lo:hi]
        left = jnp.where(rows == cols, jnp.float32(1), jnp.float32(0))
        for j in range(BLOCK - 1):
            ratio = jnp.where(rows[:, :1] > j, block[:, j : j + 1] / block[j : j + 1, j : j + 1], 0.0)
            block, left = (block - ratio * block[j : j + 1, :], left - ratio * left[j : j + 1, :])
        pivots = jnp.sum(jnp.where(rows == cols, block, 0.0), axis=1, keepdims=True)
        left = left / jnp.sqrt(pivots)
        panel = jnp.dot(left, work[lo:hi, :], precision=HIGHEST, preferred_element_type=jnp.float32)
        row_index = lax.broadcasted_iota(jnp.int32, (BLOCK, size), 0) + lo
        col_index = lax.broadcasted_iota(jnp.int32, (BLOCK, size), 1)
        top = jnp.where(col_index >= row_index, panel[:, :size], 0.0)
        upper[lo:hi, :] = top
        inverse[lo:hi, :] = panel[:, size:]
        if hi < size:
            keep = hi // TILE * TILE
            update = lax.dot_general(
                top[:, keep:], panel, (((0,), (0,)), ((), ())),
                precision=HIGHEST, preferred_element_type=jnp.float32,
            )
            work[hi:, :] = work[hi:, :] - update[hi - keep :, :]
    factor_ref[...] = upper[:, pl.ds(pl.multiple_of(c * half, TILE), half)] * (1.0 / scale)
    share = inverse[pl.ds(pl.multiple_of(c * half, TILE), half), :] * scale

    def one(i, carry):
        spot = pl.multiple_of(i * PAIR, PAIR)
        part = jnp.dot(
            share, both_ref[:, pl.ds(spot, PAIR)], precision=HIGHEST, preferred_element_type=jnp.float32
        )
        basis_ref[pl.ds(spot, PAIR), :] = part.T
        return carry

    lax.fori_loop(0, both_ref.shape[1] // PAIR, one, 0)


def shards(omega, neighbor_ids, degrees):
    zs, vs = lax.axis_size("row"), lax.axis_size("view")
    length, half = omega.shape
    slots = neighbor_ids.shape[1]
    own = length // (2 * vs)
    wide = own + 2 * HALO
    size = 2 * half
    vmem = pl.BlockSpec(memory_space=pltpu.VMEM)
    anywhere = pl.BlockSpec(memory_space=pl.ANY)
    dma = pltpu.SemaphoreType.DMA
    both, gram = pl.pallas_call(
        functools.partial(sketch_kernel, zs, vs),
        out_shape=(
            jax.ShapeDtypeStruct((size, 2 * own), jnp.float32),
            jax.ShapeDtypeStruct((size, size), jnp.float32),
        ),
        in_specs=[anywhere] * 3,
        out_specs=(vmem, vmem),
        scratch_shapes=[
            pltpu.VMEM((2, length + 2 * HALO, half), jnp.bfloat16),
            pltpu.VMEM((vs, slots, own), jnp.int32),
            pltpu.VMEM((vs, 1, length + 2 * HALO), jnp.int32),
            pltpu.VMEM((vs, 1, wide), jnp.float32),
            pltpu.VMEM((vs, own // PAIR, SPAN, PAIR), jnp.bfloat16),
            pltpu.VMEM((vs, size, wide), jnp.bfloat16),
            pltpu.VMEM((size, wide), jnp.bfloat16),
            dma((3,)),
            dma((2, max(vs - 1, 1))),
            dma((2, max(vs - 1, 1))),
            dma((2, 1)),
            dma((2, 2)),
            dma((2, vs)),
            dma((2, 2)),
            dma((2, 1)),
        ],
        compiler_params=pltpu.CompilerParams(
            collective_id=0, has_side_effects=True, vmem_limit_bytes=40 * 1024 * 1024
        ),
        name="sketch",
    )(omega, neighbor_ids, degrees)
    gram = lax.psum(gram, ("row", "view", "col"))
    return pl.pallas_call(
        functools.partial(factor_kernel, math.sqrt(length * zs)),
        out_shape=(
            jax.ShapeDtypeStruct((2 * own, half), jnp.float32),
            jax.ShapeDtypeStruct((size, half), jnp.float32),
        ),
        in_specs=[vmem, vmem],
        out_specs=(vmem, vmem),
        scratch_shapes=[
            pltpu.VMEM((size, 2 * size), jnp.float32),
            pltpu.VMEM((size, size), jnp.float32),
            pltpu.VMEM((size, size), jnp.float32),
        ],
        compiler_params=pltpu.CompilerParams(vmem_limit_bytes=32 * 1024 * 1024),
        name="factor",
    )(gram, both)


def solution(mesh):
    return jax.shard_map(
        shards,
        mesh=mesh,
        in_specs=(P("row", "col"), P("view", None, ("grp", "row")), P("view", ("grp", "row"))),
        out_specs=(P(("grp", "row", "view"), "col"), P("grp", "col")),
        check_vma=False,
    )
```

```python
import functools
import math

import jax
import jax.numpy as jnp
from jax import lax
from jax.experimental import pallas as pl
from jax.experimental.pallas import tpu as pltpu
from jax.sharding import PartitionSpec as P

TILE = 128
BAND = 4
HALO = TILE * BAND
PAIR = 2 * TILE
SPAN = PAIR + 2 * HALO
FIELDS = SPAN // TILE
BLOCK = 32
MESH = pl.DeviceIdType.MESH
HIGHEST = lax.Precision.HIGHEST


def summed_inside(zs, vs):
    return 3 * TILE % (2 * zs * vs * 8) == 0


def sketch_kernel(
    zs, vs, omega_ref, ids_ref, deg_ref, both_ref, gram_ref,
    om, ids, deg, inv, counts, scaled, first, partial, arrived, pieces,
    local_sems, ids_sems, deg_sems, om_sems, edge_sems, edge_deg_sems, halo_sems, both_sems,
    half_sems, piece_sems, spread_sems, join_sems,
):
    grp, r, v, c = (lax.axis_index(a) for a in ("grp", "row", "view", "col"))
    total = zs * vs * 2
    length = omega_ref.shape[0]
    own = length // (2 * vs)
    wide = own + 2 * HALO
    slots = ids_ref.shape[1]
    half = omega_ref.shape[1]
    place = (r * vs + v) * 2 + c
    base = pl.multiple_of((v * 2 + c) * own, HALO)

    def at(index):
        return (grp, index // (2 * vs), (index // 2) % vs, index % 2)

    def remote(src, dst, sems, slot_index, device):
        return pltpu.make_async_remote_copy(
            src_ref=src, dst_ref=dst, send_sem=sems.at[0, slot_index], recv_sem=sems.at[1, slot_index],
            device_id=device, device_id_type=MESH,
        )

    own_ids = pltpu.make_async_copy(ids_ref.at[0, :, pl.ds(base, own)], ids.at[0], local_sems.at[0])
    own_deg = pltpu.make_async_copy(deg_ref, deg.at[0, :, pl.ds(HALO, length)], local_sems.at[1])
    own_om = pltpu.make_async_copy(omega_ref, om.at[c, pl.ds(HALO, length), :], local_sems.at[2])
    own_ids.start()
    own_deg.start()
    own_om.start()

    barrier = pltpu.get_barrier_semaphore()

    def greet(i, carry):
        pl.semaphore_signal(barrier, inc=1, device_id=at((place + i) % total), device_id_type=MESH)
        return carry

    lax.fori_loop(1, total, greet, 0)
    pl.semaphore_wait(barrier, total - 1)

    sends = []
    for k in range(1, vs):
        w = (v + vs - k) % vs
        there = (grp, r, w, c)
        piece = pl.multiple_of((w * 2 + c) * own, HALO)
        sends.append(remote(ids_ref.at[0, :, pl.ds(piece, own)], ids.at[k], ids_sems, k - 1, there))
        sends.append(remote(deg_ref, deg.at[k, :, pl.ds(HALO, length)], deg_sems, k - 1, there))
    window = min(wide, length)
    other_base = (v * 2 + 1 - c) * own
    start = pl.multiple_of(jnp.clip(other_base - HALO, 0, length - window), HALO)
    om_copy = remote(
        omega_ref.at[pl.ds(start, window), :], om.at[c, pl.ds(HALO + start, window), :],
        om_sems, 0, (grp, r, v, 1 - c),
    )
    my_start = pl.multiple_of(jnp.clip(base - HALO, 0, length - window), HALO)
    om_arrive = remote(
        omega_ref.at[pl.ds(start, window), :], om.at[1 - c, pl.ds(HALO + my_start, window), :],
        om_sems, 0, (grp, r, v, 1 - c),
    )
    up_ok = r < zs - 1
    down_ok = r > 0
    next_row = jnp.minimum(r + 1, zs - 1)
    prev_row = jnp.maximum(r - 1, 0)
    low, high = pl.ds(0, HALO), pl.ds(HALO + length, HALO)
    last = pl.ds(length - HALO, HALO)
    firsts = pl.ds(0, HALO)
    edge_up = remote(omega_ref.at[last, :], om.at[c, low, :], edge_sems, c, (grp, next_row, 0, 0))
    edge_down = remote(omega_ref.at[firsts, :], om.at[c, high, :], edge_sems, c, (grp, prev_row, vs - 1, 1))
    slot_up = v
    slot_down = (v + 1) % vs
    deg_up = remote(deg_ref.at[:, last], deg.at[slot_up, :, low], edge_deg_sems, slot_up, (grp, next_row, 0, 0))
    deg_down = remote(
        deg_ref.at[:, firsts], deg.at[slot_down, :, high], edge_deg_sems, slot_down, (grp, prev_row, vs - 1, 1)
    )
    send_edge_up = up_ok & (v == 0)
    send_edge_down = down_ok & (v == vs - 1)
    send_deg_up = up_ok & (c == 0)
    send_deg_down = down_ok & (c == 1)
    get_low = down_ok & (v == 0) & (c == 0)
    get_high = up_ok & (v == vs - 1) & (c == 1)

    pl.when(send_edge_up)(edge_up.start)
    pl.when(send_edge_down)(edge_down.start)
    for s in sends:
        s.start()
    pl.when(send_deg_up)(deg_up.start)
    pl.when(send_deg_down)(deg_down.start)
    om_copy.start()

    @pl.when(r == 0)
    def _():
        om[:, low, :] = jnp.zeros((2, HALO, half), om.dtype)
        deg[:, :, low] = jnp.ones((vs, 1, HALO), deg.dtype)

    @pl.when(r == zs - 1)
    def _():
        om[:, high, :] = jnp.zeros((2, HALO, half), om.dtype)
        deg[:, :, high] = jnp.ones((vs, 1, HALO), deg.dtype)

    def build(k):
        def one(d, carry):
            mine = ids[k, :, pl.ds(pl.multiple_of(d * PAIR, PAIR), PAIR)]
            lane = lax.broadcasted_iota(jnp.int32, mine.shape, 1)
            tile = (mine >> 7) + jnp.where(lane >= TILE, 1, 0)
            within = mine & (TILE - 1)
            one_a = jnp.where(tile < 8, jnp.int32(1) << (4 * jnp.minimum(tile, 7)), 0)
            one_b = jnp.where(tile >= 8, jnp.int32(1) << (4 * jnp.maximum(tile - 8, 0)), 0)
            rows = 32
            for p in range(TILE // rows):
                spot = lax.broadcasted_iota(jnp.int32, (rows, PAIR), 0) + p * rows
                acc_a = jnp.zeros((rows, PAIR), jnp.int32)
                acc_b = jnp.zeros((rows, PAIR), jnp.int32)
                for s in range(slots):
                    hit = within[s : s + 1, :] == spot
                    acc_a = acc_a + jnp.where(hit, one_a[s : s + 1, :], 0)
                    acc_b = acc_b + jnp.where(hit, one_b[s : s + 1, :], 0)
                for h in range(FIELDS):
                    acc = acc_a if h < 8 else acc_b
                    field = (acc >> (4 * (h % 8))) & 15
                    counts[k, d, h * TILE + p * rows : h * TILE + (p + 1) * rows, :] = field.astype(
                        jnp.float32
                    ).astype(jnp.bfloat16)
            return carry

        lax.fori_loop(0, own // PAIR, one, 0)

    own_ids.wait()
    build(0)
    for k in range(1, vs):
        sends[2 * (k - 1)].wait_recv()
        build(k)
    for k in range(1, vs):
        sends[2 * (k - 1) + 1].wait_recv()
    own_deg.wait()
    own_om.wait()
    om_arrive.wait_recv()

    @pl.when(get_low)
    def _():
        for h in range(2):
            remote(omega_ref.at[last, :], om.at[h, low, :], edge_sems, h, (grp, prev_row, 0, 0)).wait_recv()
        for k in range(vs):
            remote(deg_ref.at[:, last], deg.at[k, :, low], edge_deg_sems, k, (grp, prev_row, 0, 0)).wait_recv()

    @pl.when(get_high)
    def _():
        for h in range(2):
            remote(omega_ref.at[firsts, :], om.at[h, high, :], edge_sems, h, (grp, next_row, 0, 0)).wait_recv()
        for k in range(vs):
            remote(deg_ref.at[:, firsts], deg.at[k, :, high], edge_deg_sems, k, (grp, next_row, 0, 0)).wait_recv()

    for k in range(vs):
        inv[k] = 1.0 / jnp.sqrt(deg[k, :, pl.ds(base, wide)].astype(jnp.float32))

    def turn(i, carry):
        lanes = pl.ds(pl.multiple_of(i * PAIR, PAIR), PAIR)
        for h in range(2):
            part = om[h, pl.ds(pl.multiple_of(base + i * PAIR, PAIR), PAIR), :].astype(jnp.float32).T
            for k in range(vs):
                scaled[k, h * half : (h + 1) * half, lanes] = (inv[k, :, lanes] * part).astype(jnp.bfloat16)
        return carry

    lax.fori_loop(0, wide // PAIR, turn, 0)

    def product(d):
        out = None
        for k in range(vs):
            term = jnp.dot(
                scaled[k, :, pl.ds(pl.multiple_of(d * PAIR, PAIR), SPAN)], counts[k, d],
                preferred_element_type=jnp.float32,
            )
            term = inv[k, :, pl.ds(pl.multiple_of(HALO + d * PAIR, PAIR), PAIR)] * term
            out = term if out is None else out + term
        return out

    def sweep_one(d, carry):
        first[:, pl.ds(pl.multiple_of(HALO + d * PAIR, PAIR), PAIR)] = product(d).astype(jnp.bfloat16)
        return carry

    before = at(jnp.maximum(place - 1, 0))
    after = at(jnp.minimum(place + 1, total - 1))
    down = remote(first.at[:, pl.ds(HALO, HALO)], first.at[:, pl.ds(HALO + own, HALO)], halo_sems, 0, before)
    up = remote(first.at[:, pl.ds(own, HALO)], first.at[:, pl.ds(0, HALO)], halo_sems, 1, after)
    has_before, has_after = place > 0, place < total - 1

    lax.fori_loop(0, HALO // PAIR, sweep_one, 0)
    pl.when(has_before)(down.start)
    lax.fori_loop(HALO // PAIR, own // PAIR, sweep_one, 0)
    pl.when(has_after)(up.start)

    @pl.when(place == 0)
    def _():
        first[:, pl.ds(0, HALO)] = jnp.zeros((2 * half, HALO), first.dtype)

    @pl.when(place == total - 1)
    def _():
        first[:, pl.ds(HALO + own, HALO)] = jnp.zeros((2 * half, HALO), first.dtype)

    def rescale(i, carry):
        lanes = pl.ds(pl.multiple_of(i * PAIR, PAIR), PAIR)
        part = first[:, lanes].astype(jnp.float32)
        for k in range(vs):
            scaled[k, :, lanes] = (inv[k, :, lanes] * part).astype(jnp.bfloat16)
        return carry

    lax.fori_loop(HALO // PAIR, (HALO + own) // PAIR, rescale, 0)
    pl.when(has_before)(up.wait_recv)
    lax.fori_loop(0, HALO // PAIR, rescale, 0)
    pl.when(has_after)(down.wait_recv)
    lax.fori_loop((HALO + own) // PAIR, wide // PAIR, rescale, 0)

    def sweep_two(d, carry):
        both_ref[:, pl.ds(pl.multiple_of(c * own + d * PAIR, PAIR), PAIR)] = product(d)
        return carry

    lax.fori_loop(0, own // PAIR, sweep_two, 0)
    mine = pl.ds(pl.multiple_of(c * own, PAIR), own)
    theirs = pl.ds(pl.multiple_of((1 - c) * own, PAIR), own)
    swap = remote(both_ref.at[:, mine], both_ref.at[:, mine], both_sems, 0, (grp, r, v, 1 - c))
    swap_in = remote(both_ref.at[:, mine], both_ref.at[:, theirs], both_sems, 0, (grp, r, v, 1 - c))
    swap.start()

    target = partial if summed_inside(zs, vs) else gram_ref
    inner = (((1,), (1,)), ((), ()))
    left, right = both_ref[:half, mine], both_ref[half:, mine]
    for i, (x, y) in enumerate(((left, left), (left, right), (right, right))):
        target[i * half : (i + 1) * half, :] = lax.dot_general(
            x, y, inner, precision=HIGHEST, preferred_element_type=jnp.float32
        )
    late = []
    if summed_inside(zs, vs):
        peers = zs * vs
        share = 3 * half // 2
        piece = share // peers
        spot = r * vs + v
        other = (grp, r, v, 1 - c)
        own_share = pl.multiple_of(c * share, 8)
        other_share = pl.multiple_of((1 - c) * share, 8)
        cross = remote(partial.at[pl.ds(other_share, share), :], arrived, half_sems, 0, other)
        cross.start()
        cross.wait_recv()
        late.append(cross)
        partial[pl.ds(own_share, share), :] = partial[pl.ds(own_share, share), :] + arrived[...]

        def link(src, dst, sems, sent_by, to):
            return pltpu.make_async_remote_copy(
                src_ref=src, dst_ref=dst, send_sem=sems.at[0, to], recv_sem=sems.at[1, sent_by],
                device_id=(grp, to // vs, to % vs, c), device_id_type=MESH,
            )

        for i in range(1, peers):
            to = (spot + i) % peers
            rows = pl.ds(pl.multiple_of(own_share + to * piece, 8), piece)
            copy = link(partial.at[rows, :], pieces.at[spot], piece_sems, spot, to)
            copy.start()
            late.append(copy)
        own_rows = pl.ds(pl.multiple_of(own_share + spot * piece, 8), piece)
        pieces[spot] = partial[own_rows, :]
        for i in range(1, peers):
            source = (spot + i) % peers
            link(partial.at[own_rows, :], pieces.at[source], piece_sems, source, source).wait_recv()
        whole = pieces[0]
        for i in range(1, peers):
            whole = whole + pieces[i]
        gram_ref[own_rows, :] = whole
        for i in range(1, peers):
            copy = link(gram_ref.at[own_rows, :], gram_ref.at[own_rows, :], spread_sems, spot, (spot + i) % peers)
            copy.start()
            late.append(copy)
        for i in range(1, peers):
            source = (spot + i) % peers
            rows = pl.ds(pl.multiple_of(own_share + source * piece, 8), piece)
            link(gram_ref.at[own_rows, :], gram_ref.at[rows, :], spread_sems, source, source).wait_recv()
        rows = pl.ds(own_share, share)
        join = remote(gram_ref.at[rows, :], gram_ref.at[rows, :], join_sems, 0, other)
        join.start()
        remote(gram_ref.at[rows, :], gram_ref.at[pl.ds(other_share, share), :], join_sems, 0, other).wait_recv()
        late.append(join)

    swap.wait_send()
    swap_in.wait_recv()
    for s in sends + late:
        s.wait_send()
    om_copy.wait_send()
    pl.when(send_edge_up)(edge_up.wait_send)
    pl.when(send_edge_down)(edge_down.wait_send)
    pl.when(send_deg_up)(deg_up.wait_send)
    pl.when(send_deg_down)(deg_down.wait_send)
    pl.when(has_before)(down.wait_send)
    pl.when(has_after)(up.wait_send)


def factor_kernel(scale, gram_ref, both_ref, basis_ref, factor_ref, work, upper, inverse):
    size = 2 * gram_ref.shape[1]
    c = lax.axis_index("col")
    half = size // 2
    work[:half, :half] = gram_ref[:half, :]
    work[:half, half:size] = gram_ref[half : 2 * half, :]
    work[half:, :half] = jnp.zeros((half, half), jnp.float32)
    work[half:, half:size] = gram_ref[2 * half :, :]
    work[:, size:] = jnp.where(
        lax.broadcasted_iota(jnp.int32, (size, size), 0) == lax.broadcasted_iota(jnp.int32, (size, size), 1),
        jnp.float32(1), jnp.float32(0),
    )
    rows = lax.broadcasted_iota(jnp.int32, (BLOCK, BLOCK), 0)
    cols = lax.broadcasted_iota(jnp.int32, (BLOCK, BLOCK), 1)
    for k in range(size // BLOCK):
        lo, hi = k * BLOCK, (k + 1) * BLOCK
        block = work[lo:hi, lo:hi]
        left = jnp.where(rows == cols, jnp.float32(1), jnp.float32(0))
        for j in range(BLOCK - 1):
            ratio = jnp.where(rows[:, :1] > j, block[:, j : j + 1] / block[j : j + 1, j : j + 1], 0.0)
            block, left = (block - ratio * block[j : j + 1, :], left - ratio * left[j : j + 1, :])
        pivots = jnp.sum(jnp.where(rows == cols, block, 0.0), axis=1, keepdims=True)
        left = left / jnp.sqrt(pivots)
        panel = jnp.dot(left, work[lo:hi, :], precision=HIGHEST, preferred_element_type=jnp.float32)
        row_index = lax.broadcasted_iota(jnp.int32, (BLOCK, size), 0) + lo
        col_index = lax.broadcasted_iota(jnp.int32, (BLOCK, size), 1)
        top = jnp.where(col_index >= row_index, panel[:, :size], 0.0)
        upper[lo:hi, :] = top
        inverse[lo:hi, :] = panel[:, size:]
        if hi < size:
            keep = hi // TILE * TILE
            update = lax.dot_general(
                top[:, keep:], panel, (((0,), (0,)), ((), ())),
                precision=HIGHEST, preferred_element_type=jnp.float32,
            )
            work[hi:, :] = work[hi:, :] - update[hi - keep :, :]
    factor_ref[...] = upper[:, pl.ds(pl.multiple_of(c * half, TILE), half)] * (1.0 / scale)
    share = inverse[pl.ds(pl.multiple_of(c * half, TILE), half), :] * scale

    def one(i, carry):
        spot = pl.multiple_of(i * PAIR, PAIR)
        part = jnp.dot(
            share, both_ref[:, pl.ds(spot, PAIR)], precision=HIGHEST, preferred_element_type=jnp.float32
        )
        basis_ref[pl.ds(spot, PAIR), :] = part.T
        return carry

    lax.fori_loop(0, both_ref.shape[1] // PAIR, one, 0)


def shards(omega, neighbor_ids, degrees):
    zs, vs = lax.axis_size("row"), lax.axis_size("view")
    length, half = omega.shape
    slots = neighbor_ids.shape[1]
    own = length // (2 * vs)
    wide = own + 2 * HALO
    size = 2 * half
    peers = zs * vs
    vmem = pl.BlockSpec(memory_space=pltpu.VMEM)
    anywhere = pl.BlockSpec(memory_space=pl.ANY)
    dma = pltpu.SemaphoreType.DMA
    both, gram = pl.pallas_call(
        functools.partial(sketch_kernel, zs, vs),
        out_shape=(
            jax.ShapeDtypeStruct((size, 2 * own), jnp.float32),
            jax.ShapeDtypeStruct((3 * half, half), jnp.float32),
        ),
        in_specs=[anywhere] * 3,
        out_specs=(vmem, vmem),
        scratch_shapes=[
            pltpu.VMEM((2, length + 2 * HALO, half), jnp.bfloat16),
            pltpu.VMEM((vs, slots, own), jnp.int32),
            pltpu.VMEM((vs, 1, length + 2 * HALO), jnp.int32),
            pltpu.VMEM((vs, 1, wide), jnp.float32),
            pltpu.VMEM((vs, own // PAIR, SPAN, PAIR), jnp.bfloat16),
            pltpu.VMEM((vs, size, wide), jnp.bfloat16),
            pltpu.VMEM((size, wide), jnp.bfloat16),
            pltpu.VMEM((3 * half, half), jnp.float32),
            pltpu.VMEM((3 * half // 2, half), jnp.float32),
            pltpu.VMEM((peers, max(3 * half // 2 // peers, 1), half), jnp.float32),
            dma((3,)),
            dma((2, max(vs - 1, 1))),
            dma((2, max(vs - 1, 1))),
            dma((2, 1)),
            dma((2, 2)),
            dma((2, vs)),
            dma((2, 2)),
            dma((2, 1)),
            dma((2, 1)),
            dma((2, peers)),
            dma((2, peers)),
            dma((2, 1)),
        ],
        compiler_params=pltpu.CompilerParams(
            collective_id=0, has_side_effects=True, vmem_limit_bytes=40 * 1024 * 1024
        ),
        name="sketch",
    )(omega, neighbor_ids, degrees)
    if not summed_inside(zs, vs):
        gram = lax.psum(gram, ("row", "view", "col"))
    return pl.pallas_call(
        functools.partial(factor_kernel, math.sqrt(length * zs)),
        out_shape=(
            jax.ShapeDtypeStruct((2 * own, half), jnp.float32),
            jax.ShapeDtypeStruct((size, half), jnp.float32),
        ),
        in_specs=[vmem, vmem],
        out_specs=(vmem, vmem),
        scratch_shapes=[
            pltpu.VMEM((size, 2 * size), jnp.float32),
            pltpu.VMEM((size, size), jnp.float32),
            pltpu.VMEM((size, size), jnp.float32),
        ],
        compiler_params=pltpu.CompilerParams(vmem_limit_bytes=32 * 1024 * 1024),
        name="factor",
    )(gram, both)


def solution(mesh):
    return jax.shard_map(
        shards,
        mesh=mesh,
        in_specs=(P("row", "col"), P("view", None, ("grp", "row")), P("view", ("grp", "row"))),
        out_specs=(P(("grp", "row", "view"), "col"), P("grp", "col")),
        check_vma=False,
    )
```

```python
import functools
import math

import jax
import jax.numpy as jnp
from jax import lax
from jax.experimental import pallas as pl
from jax.experimental.pallas import tpu as pltpu
from jax.sharding import PartitionSpec as P

TILE = 128
BAND = 4
HALO = TILE * BAND
PAIR = 2 * TILE
SPAN = PAIR + 2 * HALO
FIELDS = SPAN // TILE
BLOCK = 64
PANEL = 16
MESH = pl.DeviceIdType.MESH
HIGHEST = lax.Precision.HIGHEST


def summed_inside(zs, vs):
    return 3 * TILE % (2 * zs * vs * 8) == 0


def sketch_kernel(
    zs, vs, omega_ref, ids_ref, deg_ref, both_ref, gram_ref,
    om, ids, deg, inv, counts, scaled, first, partial, arrived, pieces,
    local_sems, ids_sems, deg_sems, om_sems, edge_sems, edge_deg_sems, halo_sems, both_sems,
    half_sems, piece_sems, spread_sems, join_sems,
):
    grp, r, v, c = (lax.axis_index(a) for a in ("grp", "row", "view", "col"))
    total = zs * vs * 2
    length = omega_ref.shape[0]
    own = length // (2 * vs)
    wide = own + 2 * HALO
    slots = ids_ref.shape[1]
    half = omega_ref.shape[1]
    place = (r * vs + v) * 2 + c
    base = pl.multiple_of((v * 2 + c) * own, HALO)

    def at(index):
        return (grp, index // (2 * vs), (index // 2) % vs, index % 2)

    def remote(src, dst, sems, slot_index, device):
        return pltpu.make_async_remote_copy(
            src_ref=src, dst_ref=dst, send_sem=sems.at[0, slot_index], recv_sem=sems.at[1, slot_index],
            device_id=device, device_id_type=MESH,
        )

    own_ids = pltpu.make_async_copy(ids_ref.at[0, :, pl.ds(base, own)], ids.at[0], local_sems.at[0])
    own_deg = pltpu.make_async_copy(deg_ref, deg.at[0, :, pl.ds(HALO, length)], local_sems.at[1])
    own_om = pltpu.make_async_copy(omega_ref, om.at[c, pl.ds(HALO, length), :], local_sems.at[2])
    own_ids.start()
    own_deg.start()
    own_om.start()

    barrier = pltpu.get_barrier_semaphore()

    def greet(i, carry):
        pl.semaphore_signal(barrier, inc=1, device_id=at((place + i) % total), device_id_type=MESH)
        return carry

    lax.fori_loop(1, total, greet, 0)
    pl.semaphore_wait(barrier, total - 1)

    sends = []
    for k in range(1, vs):
        w = (v + vs - k) % vs
        there = (grp, r, w, c)
        piece = pl.multiple_of((w * 2 + c) * own, HALO)
        sends.append(remote(ids_ref.at[0, :, pl.ds(piece, own)], ids.at[k], ids_sems, k - 1, there))
        sends.append(remote(deg_ref, deg.at[k, :, pl.ds(HALO, length)], deg_sems, k - 1, there))
    window = min(wide, length)
    other_base = (v * 2 + 1 - c) * own
    start = pl.multiple_of(jnp.clip(other_base - HALO, 0, length - window), HALO)
    om_copy = remote(
        omega_ref.at[pl.ds(start, window), :], om.at[c, pl.ds(HALO + start, window), :],
        om_sems, 0, (grp, r, v, 1 - c),
    )
    my_start = pl.multiple_of(jnp.clip(base - HALO, 0, length - window), HALO)
    om_arrive = remote(
        omega_ref.at[pl.ds(start, window), :], om.at[1 - c, pl.ds(HALO + my_start, window), :],
        om_sems, 0, (grp, r, v, 1 - c),
    )
    up_ok = r < zs - 1
    down_ok = r > 0
    next_row = jnp.minimum(r + 1, zs - 1)
    prev_row = jnp.maximum(r - 1, 0)
    low, high = pl.ds(0, HALO), pl.ds(HALO + length, HALO)
    last = pl.ds(length - HALO, HALO)
    firsts = pl.ds(0, HALO)
    edge_up = remote(omega_ref.at[last, :], om.at[c, low, :], edge_sems, c, (grp, next_row, 0, 0))
    edge_down = remote(omega_ref.at[firsts, :], om.at[c, high, :], edge_sems, c, (grp, prev_row, vs - 1, 1))
    slot_up = v
    slot_down = (v + 1) % vs
    deg_up = remote(deg_ref.at[:, last], deg.at[slot_up, :, low], edge_deg_sems, slot_up, (grp, next_row, 0, 0))
    deg_down = remote(
        deg_ref.at[:, firsts], deg.at[slot_down, :, high], edge_deg_sems, slot_down, (grp, prev_row, vs - 1, 1)
    )
    send_edge_up = up_ok & (v == 0)
    send_edge_down = down_ok & (v == vs - 1)
    send_deg_up = up_ok & (c == 0)
    send_deg_down = down_ok & (c == 1)
    get_low = down_ok & (v == 0) & (c == 0)
    get_high = up_ok & (v == vs - 1) & (c == 1)

    pl.when(send_edge_up)(edge_up.start)
    pl.when(send_edge_down)(edge_down.start)
    for s in sends:
        s.start()
    pl.when(send_deg_up)(deg_up.start)
    pl.when(send_deg_down)(deg_down.start)
    om_copy.start()

    @pl.when(r == 0)
    def _():
        om[:, low, :] = jnp.zeros((2, HALO, half), om.dtype)
        deg[:, :, low] = jnp.ones((vs, 1, HALO), deg.dtype)

    @pl.when(r == zs - 1)
    def _():
        om[:, high, :] = jnp.zeros((2, HALO, half), om.dtype)
        deg[:, :, high] = jnp.ones((vs, 1, HALO), deg.dtype)

    def build(k):
        def one(d, carry):
            mine = ids[k, :, pl.ds(pl.multiple_of(d * PAIR, PAIR), PAIR)]
            lane = lax.broadcasted_iota(jnp.int32, mine.shape, 1)
            tile = (mine >> 7) + jnp.where(lane >= TILE, 1, 0)
            within = mine & (TILE - 1)
            one_a = jnp.where(tile < 8, jnp.int32(1) << (4 * jnp.minimum(tile, 7)), 0)
            one_b = jnp.where(tile >= 8, jnp.int32(1) << (4 * jnp.maximum(tile - 8, 0)), 0)
            rows = 32
            for p in range(TILE // rows):
                spot = lax.broadcasted_iota(jnp.int32, (rows, PAIR), 0) + p * rows
                acc_a = jnp.zeros((rows, PAIR), jnp.int32)
                acc_b = jnp.zeros((rows, PAIR), jnp.int32)
                for s in range(slots):
                    hit = within[s : s + 1, :] == spot
                    acc_a = acc_a + jnp.where(hit, one_a[s : s + 1, :], 0)
                    acc_b = acc_b + jnp.where(hit, one_b[s : s + 1, :], 0)
                for h in range(FIELDS):
                    acc = acc_a if h < 8 else acc_b
                    field = (acc >> (4 * (h % 8))) & 15
                    counts[k, d, h * TILE + p * rows : h * TILE + (p + 1) * rows, :] = field.astype(
                        jnp.float32
                    ).astype(jnp.bfloat16)
            return carry

        lax.fori_loop(0, own // PAIR, one, 0)

    own_ids.wait()
    build(0)
    for k in range(1, vs):
        sends[2 * (k - 1)].wait_recv()
        build(k)
    for k in range(1, vs):
        sends[2 * (k - 1) + 1].wait_recv()
    own_deg.wait()
    own_om.wait()
    om_arrive.wait_recv()

    @pl.when(get_low)
    def _():
        for h in range(2):
            remote(omega_ref.at[last, :], om.at[h, low, :], edge_sems, h, (grp, prev_row, 0, 0)).wait_recv()
        for k in range(vs):
            remote(deg_ref.at[:, last], deg.at[k, :, low], edge_deg_sems, k, (grp, prev_row, 0, 0)).wait_recv()

    @pl.when(get_high)
    def _():
        for h in range(2):
            remote(omega_ref.at[firsts, :], om.at[h, high, :], edge_sems, h, (grp, next_row, 0, 0)).wait_recv()
        for k in range(vs):
            remote(deg_ref.at[:, firsts], deg.at[k, :, high], edge_deg_sems, k, (grp, next_row, 0, 0)).wait_recv()

    for k in range(vs):
        inv[k] = 1.0 / jnp.sqrt(deg[k, :, pl.ds(base, wide)].astype(jnp.float32))

    def turn(i, carry):
        lanes = pl.ds(pl.multiple_of(i * PAIR, PAIR), PAIR)
        for h in range(2):
            part = om[h, pl.ds(pl.multiple_of(base + i * PAIR, PAIR), PAIR), :].astype(jnp.float32).T
            for k in range(vs):
                scaled[k, h * half : (h + 1) * half, lanes] = (inv[k, :, lanes] * part).astype(jnp.bfloat16)
        return carry

    lax.fori_loop(0, wide // PAIR, turn, 0)

    def product(d):
        out = None
        for k in range(vs):
            term = jnp.dot(
                scaled[k, :, pl.ds(pl.multiple_of(d * PAIR, PAIR), SPAN)], counts[k, d],
                preferred_element_type=jnp.float32,
            )
            term = inv[k, :, pl.ds(pl.multiple_of(HALO + d * PAIR, PAIR), PAIR)] * term
            out = term if out is None else out + term
        return out

    def sweep_one(d, carry):
        first[:, pl.ds(pl.multiple_of(HALO + d * PAIR, PAIR), PAIR)] = product(d).astype(jnp.bfloat16)
        return carry

    before = at(jnp.maximum(place - 1, 0))
    after = at(jnp.minimum(place + 1, total - 1))
    down = remote(first.at[:, pl.ds(HALO, HALO)], first.at[:, pl.ds(HALO + own, HALO)], halo_sems, 0, before)
    up = remote(first.at[:, pl.ds(own, HALO)], first.at[:, pl.ds(0, HALO)], halo_sems, 1, after)
    has_before, has_after = place > 0, place < total - 1

    lax.fori_loop(0, HALO // PAIR, sweep_one, 0)
    pl.when(has_before)(down.start)
    lax.fori_loop(HALO // PAIR, own // PAIR, sweep_one, 0)
    pl.when(has_after)(up.start)

    @pl.when(place == 0)
    def _():
        first[:, pl.ds(0, HALO)] = jnp.zeros((2 * half, HALO), first.dtype)

    @pl.when(place == total - 1)
    def _():
        first[:, pl.ds(HALO + own, HALO)] = jnp.zeros((2 * half, HALO), first.dtype)

    def rescale(i, carry):
        lanes = pl.ds(pl.multiple_of(i * PAIR, PAIR), PAIR)
        part = first[:, lanes].astype(jnp.float32)
        for k in range(vs):
            scaled[k, :, lanes] = (inv[k, :, lanes] * part).astype(jnp.bfloat16)
        return carry

    lax.fori_loop(HALO // PAIR, (HALO + own) // PAIR, rescale, 0)
    pl.when(has_before)(up.wait_recv)
    lax.fori_loop(0, HALO // PAIR, rescale, 0)
    pl.when(has_after)(down.wait_recv)
    lax.fori_loop((HALO + own) // PAIR, wide // PAIR, rescale, 0)

    def sweep_two(d, carry):
        both_ref[:, pl.ds(pl.multiple_of(c * own + d * PAIR, PAIR), PAIR)] = product(d)
        return carry

    lax.fori_loop(0, own // PAIR, sweep_two, 0)
    mine = pl.ds(pl.multiple_of(c * own, PAIR), own)
    theirs = pl.ds(pl.multiple_of((1 - c) * own, PAIR), own)
    swap = remote(both_ref.at[:, mine], both_ref.at[:, mine], both_sems, 0, (grp, r, v, 1 - c))
    swap_in = remote(both_ref.at[:, mine], both_ref.at[:, theirs], both_sems, 0, (grp, r, v, 1 - c))
    swap.start()

    target = partial if summed_inside(zs, vs) else gram_ref
    inner = (((1,), (1,)), ((), ()))
    left, right = both_ref[:half, mine], both_ref[half:, mine]
    for i, (x, y) in enumerate(((left, left), (left, right), (right, right))):
        target[i * half : (i + 1) * half, :] = lax.dot_general(
            x, y, inner, precision=HIGHEST, preferred_element_type=jnp.float32
        )
    late = []
    if summed_inside(zs, vs):
        peers = zs * vs
        share = 3 * half // 2
        piece = share // peers
        spot = r * vs + v
        other = (grp, r, v, 1 - c)
        own_share = pl.multiple_of(c * share, 8)
        other_share = pl.multiple_of((1 - c) * share, 8)
        cross = remote(partial.at[pl.ds(other_share, share), :], arrived, half_sems, 0, other)
        cross.start()
        cross.wait_recv()
        late.append(cross)
        partial[pl.ds(own_share, share), :] = partial[pl.ds(own_share, share), :] + arrived[...]

        def link(src, dst, sems, sent_by, to):
            return pltpu.make_async_remote_copy(
                src_ref=src, dst_ref=dst, send_sem=sems.at[0, to], recv_sem=sems.at[1, sent_by],
                device_id=(grp, to // vs, to % vs, c), device_id_type=MESH,
            )

        for i in range(1, peers):
            to = (spot + i) % peers
            rows = pl.ds(pl.multiple_of(own_share + to * piece, 8), piece)
            copy = link(partial.at[rows, :], pieces.at[spot], piece_sems, spot, to)
            copy.start()
            late.append(copy)
        own_rows = pl.ds(pl.multiple_of(own_share + spot * piece, 8), piece)
        pieces[spot] = partial[own_rows, :]
        for i in range(1, peers):
            source = (spot + i) % peers
            link(partial.at[own_rows, :], pieces.at[source], piece_sems, source, source).wait_recv()
        whole = pieces[0]
        for i in range(1, peers):
            whole = whole + pieces[i]
        gram_ref[own_rows, :] = whole
        for i in range(1, peers):
            copy = link(gram_ref.at[own_rows, :], gram_ref.at[own_rows, :], spread_sems, spot, (spot + i) % peers)
            copy.start()
            late.append(copy)
        for i in range(1, peers):
            source = (spot + i) % peers
            rows = pl.ds(pl.multiple_of(own_share + source * piece, 8), piece)
            link(gram_ref.at[own_rows, :], gram_ref.at[rows, :], spread_sems, source, source).wait_recv()
        rows = pl.ds(own_share, share)
        join = remote(gram_ref.at[rows, :], gram_ref.at[rows, :], join_sems, 0, other)
        join.start()
        remote(gram_ref.at[rows, :], gram_ref.at[pl.ds(other_share, share), :], join_sems, 0, other).wait_recv()
        late.append(join)

    swap.wait_send()
    swap_in.wait_recv()
    for s in sends + late:
        s.wait_send()
    om_copy.wait_send()
    pl.when(send_edge_up)(edge_up.wait_send)
    pl.when(send_edge_down)(edge_down.wait_send)
    pl.when(send_deg_up)(deg_up.wait_send)
    pl.when(send_deg_down)(deg_down.wait_send)
    pl.when(has_before)(down.wait_send)
    pl.when(has_after)(up.wait_send)


def factor_kernel(scale, gram_ref, both_ref, basis_ref, factor_ref, work, upper, inverse):
    size = 2 * gram_ref.shape[1]
    c = lax.axis_index("col")
    half = size // 2
    work[:half, :half] = gram_ref[:half, :]
    work[:half, half:size] = gram_ref[half : 2 * half, :]
    work[half:, :half] = jnp.zeros((half, half), jnp.float32)
    work[half:, half:size] = gram_ref[2 * half :, :]
    work[:, size:] = jnp.where(
        lax.broadcasted_iota(jnp.int32, (size, size), 0) == lax.broadcasted_iota(jnp.int32, (size, size), 1),
        jnp.float32(1), jnp.float32(0),
    )
    rows = lax.broadcasted_iota(jnp.int32, (BLOCK, BLOCK), 0)
    cols = lax.broadcasted_iota(jnp.int32, (BLOCK, BLOCK), 1)
    for k in range(size // BLOCK):
        lo, hi = k * BLOCK, (k + 1) * BLOCK
        block = work[lo:hi, lo:hi]
        left = jnp.where(rows == cols, jnp.float32(1), jnp.float32(0))
        for first in range(0, BLOCK, PANEL):
            spread = [
                jnp.broadcast_to(block[:, first + i : first + i + 1], (BLOCK, BLOCK)) for i in range(PANEL)
            ]
            for i in range(PANEL):
                j = first + i
                if j == BLOCK - 1:
                    break
                ratio = jnp.where(rows > j, spread[i] * (1.0 / spread[i][j : j + 1, :]), 0.0)
                for later in range(i + 1, PANEL):
                    spread[later] = spread[later] - ratio * spread[later][j : j + 1, :]
                block, left = (block - ratio * block[j : j + 1, :], left - ratio * left[j : j + 1, :])
        pivots = jnp.sum(jnp.where(rows == cols, block, 0.0), axis=1, keepdims=True)
        left = left / jnp.sqrt(pivots)
        panel = jnp.dot(left, work[lo:hi, :], precision=HIGHEST, preferred_element_type=jnp.float32)
        row_index = lax.broadcasted_iota(jnp.int32, (BLOCK, size), 0) + lo
        col_index = lax.broadcasted_iota(jnp.int32, (BLOCK, size), 1)
        top = jnp.where(col_index >= row_index, panel[:, :size], 0.0)
        upper[lo:hi, :] = top
        inverse[lo:hi, :] = panel[:, size:]
        if hi < size:
            keep = hi // TILE * TILE
            update = lax.dot_general(
                top[:, keep:], panel, (((0,), (0,)), ((), ())),
                precision=HIGHEST, preferred_element_type=jnp.float32,
            )
            work[hi:, :] = work[hi:, :] - update[hi - keep :, :]
    factor_ref[...] = upper[:, pl.ds(pl.multiple_of(c * half, TILE), half)] * (1.0 / scale)
    share = inverse[pl.ds(pl.multiple_of(c * half, TILE), half), :] * scale

    def one(i, carry):
        spot = pl.multiple_of(i * PAIR, PAIR)
        part = jnp.dot(
            share, both_ref[:, pl.ds(spot, PAIR)], precision=HIGHEST, preferred_element_type=jnp.float32
        )
        basis_ref[pl.ds(spot, PAIR), :] = part.T
        return carry

    lax.fori_loop(0, both_ref.shape[1] // PAIR, one, 0)


def shards(omega, neighbor_ids, degrees):
    zs, vs = lax.axis_size("row"), lax.axis_size("view")
    length, half = omega.shape
    slots = neighbor_ids.shape[1]
    own = length // (2 * vs)
    wide = own + 2 * HALO
    size = 2 * half
    peers = zs * vs
    vmem = pl.BlockSpec(memory_space=pltpu.VMEM)
    anywhere = pl.BlockSpec(memory_space=pl.ANY)
    dma = pltpu.SemaphoreType.DMA
    both, gram = pl.pallas_call(
        functools.partial(sketch_kernel, zs, vs),
        out_shape=(
            jax.ShapeDtypeStruct((size, 2 * own), jnp.float32),
            jax.ShapeDtypeStruct((3 * half, half), jnp.float32),
        ),
        in_specs=[anywhere] * 3,
        out_specs=(vmem, vmem),
        scratch_shapes=[
            pltpu.VMEM((2, length + 2 * HALO, half), jnp.bfloat16),
            pltpu.VMEM((vs, slots, own), jnp.int32),
            pltpu.VMEM((vs, 1, length + 2 * HALO), jnp.int32),
            pltpu.VMEM((vs, 1, wide), jnp.float32),
            pltpu.VMEM((vs, own // PAIR, SPAN, PAIR), jnp.bfloat16),
            pltpu.VMEM((vs, size, wide), jnp.bfloat16),
            pltpu.VMEM((size, wide), jnp.bfloat16),
            pltpu.VMEM((3 * half, half), jnp.float32),
            pltpu.VMEM((3 * half // 2, half), jnp.float32),
            pltpu.VMEM((peers, max(3 * half // 2 // peers, 1), half), jnp.float32),
            dma((3,)),
            dma((2, max(vs - 1, 1))),
            dma((2, max(vs - 1, 1))),
            dma((2, 1)),
            dma((2, 2)),
            dma((2, vs)),
            dma((2, 2)),
            dma((2, 1)),
            dma((2, 1)),
            dma((2, peers)),
            dma((2, peers)),
            dma((2, 1)),
        ],
        compiler_params=pltpu.CompilerParams(
            collective_id=0, has_side_effects=True, vmem_limit_bytes=40 * 1024 * 1024
        ),
        name="sketch",
    )(omega, neighbor_ids, degrees)
    if not summed_inside(zs, vs):
        gram = lax.psum(gram, ("row", "view", "col"))
    return pl.pallas_call(
        functools.partial(factor_kernel, math.sqrt(length * zs)),
        out_shape=(
            jax.ShapeDtypeStruct((2 * own, half), jnp.float32),
            jax.ShapeDtypeStruct((size, half), jnp.float32),
        ),
        in_specs=[vmem, vmem],
        out_specs=(vmem, vmem),
        scratch_shapes=[
            pltpu.VMEM((size, 2 * size), jnp.float32),
            pltpu.VMEM((size, size), jnp.float32),
            pltpu.VMEM((size, size), jnp.float32),
        ],
        compiler_params=pltpu.CompilerParams(vmem_limit_bytes=32 * 1024 * 1024),
        name="factor",
    )(gram, both)


def solution(mesh):
    return jax.shard_map(
        shards,
        mesh=mesh,
        in_specs=(P("row", "col"), P("view", None, ("grp", "row")), P("view", ("grp", "row"))),
        out_specs=(P(("grp", "row", "view"), "col"), P("grp", "col")),
        check_vma=False,
    )
```

```python
import functools
import math

import jax
import jax.numpy as jnp
from jax import lax
from jax.experimental import pallas as pl
from jax.experimental.pallas import tpu as pltpu
from jax.sharding import PartitionSpec as P

TILE = 128
BAND = 4
HALO = TILE * BAND
PAIR = 2 * TILE
SPAN = PAIR + 2 * HALO
FIELDS = SPAN // TILE
BLOCK = 64
PANEL = 16
MESH = pl.DeviceIdType.MESH
HIGHEST = lax.Precision.HIGHEST


def summed_inside(zs, vs):
    return 3 * TILE % (2 * zs * vs * 8) == 0


def sketch_kernel(
    zs, vs, omega_ref, ids_ref, deg_ref, both_ref, gram_ref,
    om, ids, deg, inv, counts, scaled, first, partial, arrived, pieces,
    local_sems, ids_sems, deg_sems, om_sems, edge_sems, edge_deg_sems, halo_sems, both_sems,
    half_sems, piece_sems, spread_sems, join_sems,
):
    grp, r, v, c = (lax.axis_index(a) for a in ("grp", "row", "view", "col"))
    total = zs * vs * 2
    length = omega_ref.shape[0]
    own = length // (2 * vs)
    wide = own + 2 * HALO
    slots = ids_ref.shape[1]
    half = omega_ref.shape[1]
    place = (r * vs + v) * 2 + c
    base = pl.multiple_of((v * 2 + c) * own, HALO)

    def at(index):
        return (grp, index // (2 * vs), (index // 2) % vs, index % 2)

    def remote(src, dst, sems, slot_index, device):
        return pltpu.make_async_remote_copy(
            src_ref=src, dst_ref=dst, send_sem=sems.at[0, slot_index], recv_sem=sems.at[1, slot_index],
            device_id=device, device_id_type=MESH,
        )

    own_ids = pltpu.make_async_copy(ids_ref.at[0, :, pl.ds(base, own)], ids.at[0], local_sems.at[0])
    own_deg = pltpu.make_async_copy(deg_ref, deg.at[0, :, pl.ds(HALO, length)], local_sems.at[1])
    own_om = pltpu.make_async_copy(omega_ref, om.at[c, pl.ds(HALO, length), :], local_sems.at[2])
    own_ids.start()
    own_deg.start()
    own_om.start()

    barrier = pltpu.get_barrier_semaphore()

    def greet(i, carry):
        pl.semaphore_signal(barrier, inc=1, device_id=at((place + i) % total), device_id_type=MESH)
        return carry

    lax.fori_loop(1, total, greet, 0)
    pl.semaphore_wait(barrier, total - 1)

    sends = []
    for k in range(1, vs):
        w = (v + vs - k) % vs
        there = (grp, r, w, c)
        piece = pl.multiple_of((w * 2 + c) * own, HALO)
        sends.append(remote(ids_ref.at[0, :, pl.ds(piece, own)], ids.at[k], ids_sems, k - 1, there))
        sends.append(remote(deg_ref, deg.at[k, :, pl.ds(HALO, length)], deg_sems, k - 1, there))
    window = min(wide, length)
    other_base = (v * 2 + 1 - c) * own
    start = pl.multiple_of(jnp.clip(other_base - HALO, 0, length - window), HALO)
    om_copy = remote(
        omega_ref.at[pl.ds(start, window), :], om.at[c, pl.ds(HALO + start, window), :],
        om_sems, 0, (grp, r, v, 1 - c),
    )
    my_start = pl.multiple_of(jnp.clip(base - HALO, 0, length - window), HALO)
    om_arrive = remote(
        omega_ref.at[pl.ds(start, window), :], om.at[1 - c, pl.ds(HALO + my_start, window), :],
        om_sems, 0, (grp, r, v, 1 - c),
    )
    up_ok = r < zs - 1
    down_ok = r > 0
    next_row = jnp.minimum(r + 1, zs - 1)
    prev_row = jnp.maximum(r - 1, 0)
    low, high = pl.ds(0, HALO), pl.ds(HALO + length, HALO)
    last = pl.ds(length - HALO, HALO)
    firsts = pl.ds(0, HALO)
    edge_up = remote(omega_ref.at[last, :], om.at[c, low, :], edge_sems, c, (grp, next_row, 0, 0))
    edge_down = remote(omega_ref.at[firsts, :], om.at[c, high, :], edge_sems, c, (grp, prev_row, vs - 1, 1))
    slot_up = v
    slot_down = (v + 1) % vs
    deg_up = remote(deg_ref.at[:, last], deg.at[slot_up, :, low], edge_deg_sems, slot_up, (grp, next_row, 0, 0))
    deg_down = remote(
        deg_ref.at[:, firsts], deg.at[slot_down, :, high], edge_deg_sems, slot_down, (grp, prev_row, vs - 1, 1)
    )
    send_edge_up = up_ok & (v == 0)
    send_edge_down = down_ok & (v == vs - 1)
    send_deg_up = up_ok & (c == 0)
    send_deg_down = down_ok & (c == 1)
    get_low = down_ok & (v == 0) & (c == 0)
    get_high = up_ok & (v == vs - 1) & (c == 1)

    pl.when(send_edge_up)(edge_up.start)
    pl.when(send_edge_down)(edge_down.start)
    for s in sends:
        s.start()
    pl.when(send_deg_up)(deg_up.start)
    pl.when(send_deg_down)(deg_down.start)
    om_copy.start()

    @pl.when(r == 0)
    def _():
        om[:, low, :] = jnp.zeros((2, HALO, half), om.dtype)
        deg[:, :, low] = jnp.ones((vs, 1, HALO), deg.dtype)

    @pl.when(r == zs - 1)
    def _():
        om[:, high, :] = jnp.zeros((2, HALO, half), om.dtype)
        deg[:, :, high] = jnp.ones((vs, 1, HALO), deg.dtype)

    def build(k):
        def one(d, carry):
            mine = ids[k, :, pl.ds(pl.multiple_of(d * PAIR, PAIR), PAIR)]
            lane = lax.broadcasted_iota(jnp.int32, mine.shape, 1)
            tile = (mine >> 7) + jnp.where(lane >= TILE, 1, 0)
            within = mine & (TILE - 1)
            one_a = jnp.where(tile < 8, jnp.int32(1) << (4 * jnp.minimum(tile, 7)), 0)
            one_b = jnp.where(tile >= 8, jnp.int32(1) << (4 * jnp.maximum(tile - 8, 0)), 0)
            rows = 32
            for p in range(TILE // rows):
                spot = lax.broadcasted_iota(jnp.int32, (rows, PAIR), 0) + p * rows
                acc_a = jnp.zeros((rows, PAIR), jnp.int32)
                acc_b = jnp.zeros((rows, PAIR), jnp.int32)
                for s in range(slots):
                    hit = within[s : s + 1, :] == spot
                    acc_a = acc_a + jnp.where(hit, one_a[s : s + 1, :], 0)
                    acc_b = acc_b + jnp.where(hit, one_b[s : s + 1, :], 0)
                for h in range(FIELDS):
                    acc = acc_a if h < 8 else acc_b
                    field = (acc >> (4 * (h % 8))) & 15
                    counts[k, d, h * TILE + p * rows : h * TILE + (p + 1) * rows, :] = field.astype(
                        jnp.float32
                    ).astype(jnp.bfloat16)
            return carry

        lax.fori_loop(0, own // PAIR, one, 0)

    own_ids.wait()
    build(0)
    for k in range(1, vs):
        sends[2 * (k - 1)].wait_recv()
        build(k)
    for k in range(1, vs):
        sends[2 * (k - 1) + 1].wait_recv()
    own_deg.wait()
    own_om.wait()
    om_arrive.wait_recv()

    @pl.when(get_low)
    def _():
        for h in range(2):
            remote(omega_ref.at[last, :], om.at[h, low, :], edge_sems, h, (grp, prev_row, 0, 0)).wait_recv()
        for k in range(vs):
            remote(deg_ref.at[:, last], deg.at[k, :, low], edge_deg_sems, k, (grp, prev_row, 0, 0)).wait_recv()

    @pl.when(get_high)
    def _():
        for h in range(2):
            remote(omega_ref.at[firsts, :], om.at[h, high, :], edge_sems, h, (grp, next_row, 0, 0)).wait_recv()
        for k in range(vs):
            remote(deg_ref.at[:, firsts], deg.at[k, :, high], edge_deg_sems, k, (grp, next_row, 0, 0)).wait_recv()

    for k in range(vs):
        inv[k] = 1.0 / jnp.sqrt(deg[k, :, pl.ds(base, wide)].astype(jnp.float32))

    def turn(i, carry):
        lanes = pl.ds(pl.multiple_of(i * PAIR, PAIR), PAIR)
        for h in range(2):
            part = om[h, pl.ds(pl.multiple_of(base + i * PAIR, PAIR), PAIR), :].astype(jnp.float32).T
            for k in range(vs):
                scaled[k, h * half : (h + 1) * half, lanes] = (inv[k, :, lanes] * part).astype(jnp.bfloat16)
        return carry

    lax.fori_loop(0, wide // PAIR, turn, 0)

    def product(d):
        out = None
        for k in range(vs):
            term = jnp.dot(
                scaled[k, :, pl.ds(pl.multiple_of(d * PAIR, PAIR), SPAN)], counts[k, d],
                preferred_element_type=jnp.float32,
            )
            term = inv[k, :, pl.ds(pl.multiple_of(HALO + d * PAIR, PAIR), PAIR)] * term
            out = term if out is None else out + term
        return out

    def sweep_one(d, carry):
        first[:, pl.ds(pl.multiple_of(HALO + d * PAIR, PAIR), PAIR)] = product(d).astype(jnp.bfloat16)
        return carry

    before = at(jnp.maximum(place - 1, 0))
    after = at(jnp.minimum(place + 1, total - 1))
    down = remote(first.at[:, pl.ds(HALO, HALO)], first.at[:, pl.ds(HALO + own, HALO)], halo_sems, 0, before)
    up = remote(first.at[:, pl.ds(own, HALO)], first.at[:, pl.ds(0, HALO)], halo_sems, 1, after)
    has_before, has_after = place > 0, place < total - 1

    lax.fori_loop(0, HALO // PAIR, sweep_one, 0)
    pl.when(has_before)(down.start)
    lax.fori_loop(HALO // PAIR, own // PAIR, sweep_one, 0)
    pl.when(has_after)(up.start)

    @pl.when(place == 0)
    def _():
        first[:, pl.ds(0, HALO)] = jnp.zeros((2 * half, HALO), first.dtype)

    @pl.when(place == total - 1)
    def _():
        first[:, pl.ds(HALO + own, HALO)] = jnp.zeros((2 * half, HALO), first.dtype)

    def rescale(i, carry):
        lanes = pl.ds(pl.multiple_of(i * PAIR, PAIR), PAIR)
        part = first[:, lanes].astype(jnp.float32)
        for k in range(vs):
            scaled[k, :, lanes] = (inv[k, :, lanes] * part).astype(jnp.bfloat16)
        return carry

    lax.fori_loop(HALO // PAIR, (HALO + own) // PAIR, rescale, 0)
    pl.when(has_before)(up.wait_recv)
    lax.fori_loop(0, HALO // PAIR, rescale, 0)
    pl.when(has_after)(down.wait_recv)
    lax.fori_loop((HALO + own) // PAIR, wide // PAIR, rescale, 0)

    def sweep_two(d, carry):
        both_ref[:, pl.ds(pl.multiple_of(c * own + d * PAIR, PAIR), PAIR)] = product(d)
        return carry

    lax.fori_loop(0, own // PAIR, sweep_two, 0)
    mine = pl.ds(pl.multiple_of(c * own, PAIR), own)
    theirs = pl.ds(pl.multiple_of((1 - c) * own, PAIR), own)
    swap = remote(both_ref.at[:, mine], both_ref.at[:, mine], both_sems, 0, (grp, r, v, 1 - c))
    swap_in = remote(both_ref.at[:, mine], both_ref.at[:, theirs], both_sems, 0, (grp, r, v, 1 - c))
    swap.start()

    target = partial if summed_inside(zs, vs) else gram_ref
    inner = (((1,), (1,)), ((), ()))
    left, right = both_ref[:half, mine], both_ref[half:, mine]
    for i, (x, y) in enumerate(((left, left), (left, right), (right, right))):
        target[i * half : (i + 1) * half, :] = lax.dot_general(
            x, y, inner, precision=HIGHEST, preferred_element_type=jnp.float32
        )
    late = []
    if summed_inside(zs, vs):
        peers = zs * vs
        share = 3 * half // 2
        piece = share // peers
        spot = r * vs + v
        other = (grp, r, v, 1 - c)
        own_share = pl.multiple_of(c * share, 8)
        other_share = pl.multiple_of((1 - c) * share, 8)
        cross = remote(partial.at[pl.ds(other_share, share), :], arrived, half_sems, 0, other)
        cross.start()
        cross.wait_recv()
        late.append(cross)
        partial[pl.ds(own_share, share), :] = partial[pl.ds(own_share, share), :] + arrived[...]

        def link(src, dst, sems, sent_by, to):
            return pltpu.make_async_remote_copy(
                src_ref=src, dst_ref=dst, send_sem=sems.at[0, to], recv_sem=sems.at[1, sent_by],
                device_id=(grp, to // vs, to % vs, c), device_id_type=MESH,
            )

        for i in range(1, peers):
            to = (spot + i) % peers
            rows = pl.ds(pl.multiple_of(own_share + to * piece, 8), piece)
            copy = link(partial.at[rows, :], pieces.at[spot], piece_sems, spot, to)
            copy.start()
            late.append(copy)
        own_rows = pl.ds(pl.multiple_of(own_share + spot * piece, 8), piece)
        pieces[spot] = partial[own_rows, :]
        for i in range(1, peers):
            source = (spot + i) % peers
            link(partial.at[own_rows, :], pieces.at[source], piece_sems, source, source).wait_recv()
        whole = pieces[0]
        for i in range(1, peers):
            whole = whole + pieces[i]
        gram_ref[own_rows, :] = whole
        for i in range(1, peers):
            copy = link(gram_ref.at[own_rows, :], gram_ref.at[own_rows, :], spread_sems, spot, (spot + i) % peers)
            copy.start()
            late.append(copy)
        for i in range(1, peers):
            source = (spot + i) % peers
            rows = pl.ds(pl.multiple_of(own_share + source * piece, 8), piece)
            link(gram_ref.at[own_rows, :], gram_ref.at[rows, :], spread_sems, source, source).wait_recv()
        rows = pl.ds(own_share, share)
        join = remote(gram_ref.at[rows, :], gram_ref.at[rows, :], join_sems, 0, other)
        join.start()
        remote(gram_ref.at[rows, :], gram_ref.at[pl.ds(other_share, share), :], join_sems, 0, other).wait_recv()
        late.append(join)

    swap.wait_send()
    swap_in.wait_recv()
    for s in sends + late:
        s.wait_send()
    om_copy.wait_send()
    pl.when(send_edge_up)(edge_up.wait_send)
    pl.when(send_edge_down)(edge_down.wait_send)
    pl.when(send_deg_up)(deg_up.wait_send)
    pl.when(send_deg_down)(deg_down.wait_send)
    pl.when(has_before)(down.wait_send)
    pl.when(has_after)(up.wait_send)


def factor_kernel(scale, gram_ref, both_ref, basis_ref, factor_ref, work, upper, inverse):
    size = 2 * gram_ref.shape[1]
    c = lax.axis_index("col")
    half = size // 2
    work[:half, :half] = gram_ref[:half, :]
    work[:half, half:size] = gram_ref[half : 2 * half, :]
    work[half:, :half] = jnp.zeros((half, half), jnp.float32)
    work[half:, half:size] = gram_ref[2 * half :, :]
    work[:, size:] = jnp.where(
        lax.broadcasted_iota(jnp.int32, (size, size), 0) == lax.broadcasted_iota(jnp.int32, (size, size), 1),
        jnp.float32(1), jnp.float32(0),
    )
    rows = lax.broadcasted_iota(jnp.int32, (BLOCK, BLOCK), 0)
    cols = lax.broadcasted_iota(jnp.int32, (BLOCK, BLOCK), 1)
    for k in range(size // BLOCK):
        lo, hi = k * BLOCK, (k + 1) * BLOCK
        block = work[lo:hi, lo:hi]
        left = jnp.where(rows == cols, jnp.float32(1), jnp.float32(0))
        for first in range(0, BLOCK, PANEL):
            spread = [
                jnp.broadcast_to(block[:, first + i : first + i + 1], (BLOCK, BLOCK)) for i in range(PANEL)
            ]
            for i in range(PANEL):
                j = first + i
                if j == BLOCK - 1:
                    break
                ratio = jnp.where(rows > j, spread[i] * (1.0 / spread[i][j : j + 1, :]), 0.0)
                for later in range(i + 1, PANEL):
                    spread[later] = spread[later] - ratio * spread[later][j : j + 1, :]
                block, left = (block - ratio * block[j : j + 1, :], left - ratio * left[j : j + 1, :])
        pivots = jnp.sum(jnp.where(rows == cols, block, 0.0), axis=1, keepdims=True)
        left = left / jnp.sqrt(pivots)
        panel = jnp.dot(left, work[lo:hi, :], precision=HIGHEST, preferred_element_type=jnp.float32)
        row_index = lax.broadcasted_iota(jnp.int32, (BLOCK, size), 0) + lo
        col_index = lax.broadcasted_iota(jnp.int32, (BLOCK, size), 1)
        top = jnp.where(col_index >= row_index, panel[:, :size], 0.0)
        upper[lo:hi, :] = top
        inverse[lo:hi, :] = panel[:, size:]
        if hi < size:
            keep = hi // TILE * TILE
            update = lax.dot_general(
                top[:, keep:], panel, (((0,), (0,)), ((), ())),
                precision=HIGHEST, preferred_element_type=jnp.float32,
            )
            work[hi:, :] = work[hi:, :] - update[hi - keep :, :]
    factor_ref[...] = upper[:, pl.ds(pl.multiple_of(c * half, TILE), half)] * (1.0 / scale)
    share = inverse[pl.ds(pl.multiple_of(c * half, TILE), half), :] * scale

    def one(i, carry):
        spot = pl.multiple_of(i * PAIR, PAIR)
        part = jnp.dot(
            share, both_ref[:, pl.ds(spot, PAIR)], precision=HIGHEST, preferred_element_type=jnp.float32
        )
        basis_ref[pl.ds(spot, PAIR), :] = part.T
        return carry

    lax.fori_loop(0, both_ref.shape[1] // PAIR, one, 0, unroll=True)


def shards(omega, neighbor_ids, degrees):
    zs, vs = lax.axis_size("row"), lax.axis_size("view")
    length, half = omega.shape
    slots = neighbor_ids.shape[1]
    own = length // (2 * vs)
    wide = own + 2 * HALO
    size = 2 * half
    peers = zs * vs
    vmem = pl.BlockSpec(memory_space=pltpu.VMEM)
    anywhere = pl.BlockSpec(memory_space=pl.ANY)
    dma = pltpu.SemaphoreType.DMA
    both, gram = pl.pallas_call(
        functools.partial(sketch_kernel, zs, vs),
        out_shape=(
            jax.ShapeDtypeStruct((size, 2 * own), jnp.float32),
            jax.ShapeDtypeStruct((3 * half, half), jnp.float32),
        ),
        in_specs=[anywhere] * 3,
        out_specs=(vmem, vmem),
        scratch_shapes=[
            pltpu.VMEM((2, length + 2 * HALO, half), jnp.bfloat16),
            pltpu.VMEM((vs, slots, own), jnp.int32),
            pltpu.VMEM((vs, 1, length + 2 * HALO), jnp.int32),
            pltpu.VMEM((vs, 1, wide), jnp.float32),
            pltpu.VMEM((vs, own // PAIR, SPAN, PAIR), jnp.bfloat16),
            pltpu.VMEM((vs, size, wide), jnp.bfloat16),
            pltpu.VMEM((size, wide), jnp.bfloat16),
            pltpu.VMEM((3 * half, half), jnp.float32),
            pltpu.VMEM((3 * half // 2, half), jnp.float32),
            pltpu.VMEM((peers, max(3 * half // 2 // peers, 1), half), jnp.float32),
            dma((3,)),
            dma((2, max(vs - 1, 1))),
            dma((2, max(vs - 1, 1))),
            dma((2, 1)),
            dma((2, 2)),
            dma((2, vs)),
            dma((2, 2)),
            dma((2, 1)),
            dma((2, 1)),
            dma((2, peers)),
            dma((2, peers)),
            dma((2, 1)),
        ],
        compiler_params=pltpu.CompilerParams(
            collective_id=0, has_side_effects=True, vmem_limit_bytes=40 * 1024 * 1024
        ),
        name="sketch",
    )(omega, neighbor_ids, degrees)
    if not summed_inside(zs, vs):
        gram = lax.psum(gram, ("row", "view", "col"))
    return pl.pallas_call(
        functools.partial(factor_kernel, math.sqrt(length * zs)),
        out_shape=(
            jax.ShapeDtypeStruct((2 * own, half), jnp.float32),
            jax.ShapeDtypeStruct((size, half), jnp.float32),
        ),
        in_specs=[vmem, vmem],
        out_specs=(vmem, vmem),
        scratch_shapes=[
            pltpu.VMEM((size, 2 * size), jnp.float32),
            pltpu.VMEM((size, size), jnp.float32),
            pltpu.VMEM((size, size), jnp.float32),
        ],
        compiler_params=pltpu.CompilerParams(vmem_limit_bytes=32 * 1024 * 1024),
        name="factor",
    )(gram, both)


def solution(mesh):
    return jax.shard_map(
        shards,
        mesh=mesh,
        in_specs=(P("row", "col"), P("view", None, ("grp", "row")), P("view", ("grp", "row"))),
        out_specs=(P(("grp", "row", "view"), "col"), P("grp", "col")),
        check_vma=False,
    )
```
